128 devices in a mesh: rep: 16 (over y, x_hi, core), fsdp: 8 (over z, x_lo).
Axes of the slice: x: 4 (x_hi: 2, x_lo: 2; x = x_hi * 2 + x_lo), y: 4, z: 4, core: 2. Of those that a mesh axis runs over, the one named last changes fastest.
Arguments:
- params: float32 [16, 2560, 2560], P('rep', 'fsdp'), may hold values from -6 to 6
- push_weight: float32 [16], P('rep'), may hold values from 0.5 to 2
- inbox_params: float32 [16, 2560, 2560], P('rep', 'fsdp'), may hold values from -3 to 3
- inbox_weight: float32 [16], P('rep'), may hold values from 0.25 to 1
- heads: bfloat16 [16, 3072, 2560], P('rep', 'fsdp'), may hold values from -6 to 6
- residual: bfloat16 [16, 3072, 2560], P('rep', 'fsdp'), may hold values from -40 to 40
- cotangent: bfloat16 [16, 3072, 2560], P('rep', 'fsdp'), may hold values from -6 to 6
- gain: float32 [2560], replicated, may hold values from 0.5 to 2
- offset: int32 [8], replicated, may hold values from 1 to 8, as said below
Outputs:
- new_params: float32 [16, 2560, 2560], P('rep', 'fsdp')
- new_weight: float32 [16], P('rep')
- outbox_params: float32 [16, 2560, 2560], P('rep', 'fsdp')
- outbox_weight: float32 [16], P('rep')
- grad_heads: bfloat16 [16, 3072, 2560], P('rep', 'fsdp')
The draws below stay inside these ranges and needn't reach their ends.
Inputs may be any that keep to these rules, and one draw needn't show every extreme that they name: `offset`: each entry a power of two below 16; 1 and 8 both occur in every plan.
All inputs are finite; a program needn't handle non-finite values.
Results may differ from the reference program's by a relative error of at most 0.0057.
Values may be sent and summed in bfloat16 or wider, within the bound.
A program may use at most 192 MiB of HBM per device.

```python
import math
import jax
import jax.numpy as jnp
from jax import lax

D = 2560
HEADS = 20
HEAD_DIM = 128
PLAN = 8
INNER = 2560
GROUP_TOK = 3072
REPS = 16


def draw_residual(key, part):
    key = jax.random.fold_in(key, 3)
    key_base, key_rows, key_cols = jax.random.split(key, 3)
    shape = (REPS, GROUP_TOK, D)
    base = jnp.clip(jax.random.normal(key_base, shape, jnp.float32), -4.0, 4.0)
    rows = jnp.exp(jax.random.uniform(key_rows, (REPS, GROUP_TOK, 1), jnp.float32, -1.15, 1.15))
    cols = jnp.exp(jax.random.uniform(key_cols, (1, 1, D), jnp.float32, -1.15, 1.15))
    return (base * rows * cols).astype(jnp.bfloat16)


def draw_offset(key, part):
    key = jax.random.fold_in(key, 11)
    key_levels, key_places = jax.random.split(key, 2)
    levels = REPS.bit_length() - 1
    exponent = jax.random.randint(key_levels, (PLAN,), 0, levels).astype(jnp.int32)
    places = jax.random.permutation(key_places, jnp.arange(PLAN, dtype=jnp.int32))
    positions = jnp.arange(PLAN, dtype=jnp.int32)
    exponent = jnp.where(positions == places[0], levels - 1, exponent)
    exponent = jnp.where(positions == places[1], 0, exponent).astype(jnp.int32)
    return jnp.left_shift(jnp.ones((PLAN,), jnp.int32), exponent)


def steps_of(stream_key, shape, shards, smallest, high):
    level = 1.0
    for dim, parts in shards:
        draws = jax.random.uniform(jax.random.fold_in(jax.random.fold_in(stream_key, 6), dim), (parts,), jnp.float32, smallest / len(shards), high / len(shards))
        level = level * jnp.repeat(jnp.exp(draws), shape[dim] // parts).reshape((-1,) + (1,) * (len(shape) - 1 - dim))
    return level


def normal_values(rng, extent, width, reach, cuts=(), kind=jnp.bfloat16):
    entries = jax.random.normal(rng, extent, jnp.float32) * width
    if len(cuts) > 0:
        entries = steps_of(rng, extent, cuts, -0.22, 0.18) * entries
    return jnp.clip(entries, min=-reach, max=reach).astype(kind)


def setup_inputs(seed: int = 0) -> dict:
    key_of = jax.random.split(jax.random.key(seed), 10)
    params = normal_values(key_of[0], (REPS, INNER, D), 1.0, 6.0, ((0, 16), (1, 8)), jnp.float32)
    push_weight = jnp.clip(jnp.exp(math.log(2.0) - 1.3862944 * jax.random.uniform(key_of[1], (REPS,), jnp.float32) ** steps_of(key_of[1], (REPS,), ((0, 16),), -0.2, 0.2)), 0.5, 2.0)
    inbox_params = normal_values(key_of[2], (REPS, INNER, D), 0.5, 3.0, ((0, 16), (1, 8)), jnp.float32)
    inbox_weight = jnp.clip(jnp.exp(math.log(1.0) - 1.3862944 * jax.random.uniform(key_of[3], (REPS,), jnp.float32) ** steps_of(key_of[3], (REPS,), ((0, 16),), -0.2, 0.2)), 0.25, 1.0)
    heads = normal_values(key_of[4], (REPS, GROUP_TOK, INNER), 1.0, 6.0, ((0, 16), (1, 8)))
    residual = draw_residual(jax.random.fold_in(key_of[9], 71), 0)
    cotangent = normal_values(key_of[6], (REPS, GROUP_TOK, D), 1.0, 6.0, ((0, 16), (1, 8)))
    gain = jnp.clip(jnp.exp(jax.random.uniform(key_of[7], (D,), jnp.float32, math.log(0.5), math.log(2.0))), 0.5, 2.0)
    offset = draw_offset(jax.random.fold_in(key_of[9], 71), 0)
    return dict(params=params, push_weight=push_weight, inbox_params=inbox_params, inbox_weight=inbox_weight, heads=heads, residual=residual, cotangent=cotangent, gain=gain, offset=offset)


def reference(params, push_weight, inbox_params, inbox_weight, heads, residual, cotangent, gain, offset):
    scaling = (HEADS * HEAD_DIM) ** (-0.5)

    def per_replica(replica_items):
        numer, weight_one, head_rows, resid_rows, cot_rows = replica_items
        weights = (numer / weight_one * scaling).astype(jnp.bfloat16)
        summed = resid_rows.astype(jnp.float32) + jnp.dot(head_rows, weights, preferred_element_type=jnp.float32)
        inverse = lax.rsqrt(lax.optimization_barrier(jnp.mean(summed * summed, axis=-1, keepdims=True)) + 1e-05)
        scaled_cot = gain * cot_rows.astype(jnp.float32)
        unit_grad = (inverse * scaled_cot - summed * inverse ** 3 * lax.optimization_barrier(jnp.mean(scaled_cot * summed, axis=-1, keepdims=True))).astype(jnp.bfloat16)
        grad_rows = jnp.dot(unit_grad, weights.T, preferred_element_type=jnp.float32).astype(jnp.bfloat16)
        weight_grad = jnp.dot(head_rows.T, unit_grad, preferred_element_type=jnp.float32)
        kept_half = 0.5 * (numer - 0.004 * weight_grad)
        return (kept_half, grad_rows)
    kept_half, grad_heads = lax.map(per_replica, (params, push_weight, heads, residual, cotangent))
    new_params = kept_half + inbox_params
    new_weight = 0.5 * push_weight + inbox_weight
    source = (jnp.arange(REPS, dtype=jnp.int32) - offset[0]) % REPS
    outbox_params = jnp.take(kept_half, source, axis=0)
    outbox_weight = jnp.take(0.5 * push_weight, source, axis=0)
    return (new_params, new_weight, outbox_params, outbox_weight, grad_heads)
```

```python
import functools

import jax
import jax.numpy as jnp
from jax import lax
from jax.experimental import pallas as pl
from jax.experimental.pallas import tpu as pltpu
from jax.sharding import PartitionSpec as P

MESH = pl.DeviceIdType.MESH
F32 = jnp.float32
BF16 = jnp.bfloat16

CW = 256
PIECES = 4
LEAD = 4
EPS = 1e-05


def dot(a, b):
    return jnp.dot(a, b, preferred_element_type=F32)


def dot_t(a, b):
    return lax.dot_general(a, b, (((1,), (1,)), ((), ())), preferred_element_type=F32)


def step_kernel(
    by, zs, inner,
    params, push, heads, residual, cotangent, gain,
    g_own, g_got, dw_out, outbox, w_out,
    pv, hv, rv, cv, hp, ho, ht, wb, sv, sb, srv, acc1, acc2, ub, pb, st1, st2, gacc, gb, gsend, ob, dwv, wv,
    lp, lx, hs, hr, aos, aor, afs, afr, ss, sr, us, ur, s1s, s1r, s2s, s2r, gs, gr, os_, or_, ws, wr, dws, gos,
):
    rows, cols = params.shape
    tok = heads.shape[0]
    nc = cols // CW
    half = rows // 2
    kh = zs * rows
    reps = lax.axis_size("rep")
    r = lax.axis_index("rep")
    f = lax.axis_index("fsdp")
    z, xl = f // 2, f % 2
    zp, zm, zo = (z + 1) % zs, (z + zs - 1) % zs, (z + 2) % zs
    up, down = (r, zp * 2 + xl), (r, zm * 2 + xl)
    side = (r, z * 2 + 1 - xl)
    ahead, behind = ((r + by) % reps, f), ((r + reps - by) % reps, f)
    ways = (up, down)

    def remote(src, dst, send, recv, to):
        return pltpu.make_async_remote_copy(
            src_ref=src, dst_ref=dst, send_sem=send, recv_sem=recv, device_id=to, device_id_type=MESH
        )

    def at_cols(c):
        return pl.ds(pl.multiple_of(c * CW, CW), CW)

    def at_rows(start, size):
        return pl.ds(pl.multiple_of(start, 16), size)

    def load_params(c):
        return pltpu.make_async_copy(params.at[:, at_cols(c)], pv.at[c], lp.at[c])

    load_heads = pltpu.make_async_copy(heads, hv, lx.at[0])
    load_res = pltpu.make_async_copy(residual, rv, lx.at[1])
    load_cot = pltpu.make_async_copy(cotangent, cv, lx.at[2])
    piece = tok // PIECES

    def send_heads(p):
        here = at_rows(p * piece, piece)
        there = at_rows(tok + p * piece, piece)
        return remote(ho.at[here], hp.at[there], hs.at[p], hr.at[p], side)

    def send_own(d, c):
        block = wb.at[c, at_rows(z * rows, rows)]
        return remote(block, block, aos.at[d, c], aor.at[d, c], ways[d])

    def send_on(d, c):
        start = zm * rows if d == 0 else zp * rows + half
        block = wb.at[c, at_rows(start, half)]
        return remote(block, block, afs.at[d, c], afr.at[d, c], ways[d])

    def send_sum(c):
        return remote(sb.at[c], srv.at[c], ss.at[c], sr.at[c], side)

    def send_unit(c):
        return remote(ub.at[c, pl.ds(0, tok)], ub.at[c, pl.ds(tok, tok)], us.at[c], ur.at[c], side)

    def send_far(d, c):
        block = pb.at[c, at_rows(zo * rows + d * half, half)]
        return remote(block, st1.at[d, c], s1s.at[d, c], s1r.at[d, c], ways[d])

    def send_near(d, c):
        block = pb.at[c, at_rows((zm if d else zp) * rows, rows)]
        return remote(block, st2.at[d, c], s2s.at[d, c], s2r.at[d, c], ways[d])

    def send_grad(p):
        here = at_rows(p * piece, piece)
        return remote(gsend.at[here], g_got.at[here], gs.at[p], gr.at[p], side)

    def send_out(c):
        return remote(ob.at[c], outbox.at[:, at_cols(c)], os_.at[c], or_.at[c], ahead)

    send_weight = remote(wv, w_out, ws.at[0], wr.at[0], ahead)

    def store_dw(c):
        return pltpu.make_async_copy(dwv.at[c], dw_out.at[:, at_cols(c)], dws.at[c])

    store_own = pltpu.make_async_copy(gb, g_own, gos.at[0])

    def loads(c, _):
        load_params(c).start()
        return 0

    lax.fori_loop(0, nc, loads, 0)
    load_heads.start()
    load_res.start()
    load_cot.start()

    barrier = pltpu.get_barrier_semaphore()
    for device in (up, down, side, ahead, behind):
        pl.semaphore_signal(barrier, inc=1, device_id=device, device_id_type=MESH)
    pl.semaphore_wait(barrier, 5)

    weight = push[0]
    scale = (inner ** -0.5) / jnp.full((1, CW), weight, F32)

    def own_chunk(c):
        load_params(c).wait()
        wb[c, at_rows(z * rows, rows), :] = (pv[c] * scale).astype(BF16)
        for d in range(2):
            send_own(d, c).start()

    own_chunk(0)
    load_heads.wait()

    def split_heads(p, _):
        here = at_rows(p * piece, piece)
        for side_x in range(2):

            @pl.when(xl == side_x)
            def _():
                for s in range(2 * zs):
                    dst = hp if s % 2 == side_x else ho
                    to = (s // 2) * rows
                    dst[here, to : to + rows] = hv[here, s * rows : (s + 1) * rows]

        send_heads(p).start()
        return 0

    lax.fori_loop(0, PIECES, split_heads, 0)
    own_chunk(1)
    load_res.wait()
    load_cot.wait()

    def z_step(c):
        @pl.when(c + 2 < nc)
        def _():
            own_chunk(c + 2)

        for d in range(2):
            send_own(d, c).wait_recv()
            send_on(d, c).start()

    def s_step(c):
        for d in range(2):
            send_on(d, c).wait_recv()
        sb[c] = dot(hp[tok : 2 * tok, :], wb[c]).astype(BF16)
        send_sum(c).start()
        sv[c] = dot(hp[0:tok, :], wb[c])

    def scaled(c):
        return gain[:, at_cols(c)] * cv[:, at_cols(c)].astype(F32)

    def f_step(c):
        send_sum(c).wait_recv()
        s = sv[c] + srv[c].astype(F32) + rv[:, at_cols(c)].astype(F32)
        sv[c] = s
        sq = s * s
        pr = scaled(c) * s
        a1, a2 = acc1[...], acc2[...]
        for k in range(CW // 128):
            a1 += sq[:, k * 128 : (k + 1) * 128]
            a2 += pr[:, k * 128 : (k + 1) * 128]
        acc1[...] = a1
        acc2[...] = a2

    def turn(j):
        lanes = pl.ds(pl.multiple_of(j * 128, 128), 128)
        ht[at_rows(j * 128, 128), :] = hp[:, lanes].T

    acc1[...] = jnp.zeros_like(acc1)
    acc2[...] = jnp.zeros_like(acc2)

    def lead_body(i, _):
        z_step(i)
        return 0

    lax.fori_loop(0, LEAD, lead_body, 0)
    for p in range(PIECES):
        send_heads(p).wait_recv()
    s_step(0)
    turns = kh // 128
    per = -(-turns // (nc - LEAD))

    def main_body(i, _):
        z_step(i)
        s_step(i - LEAD + 1)

        @pl.when(i >= LEAD + 2)
        def _():
            f_step(i - LEAD - 2)

        def turn_body(j, _):
            turn(j)
            return 0

        first = (i - LEAD) * per
        lax.fori_loop(first, jnp.minimum(first + per, turns), turn_body, 0)
        return 0

    lax.fori_loop(LEAD, nc, main_body, 0)

    def rest_s(c, _):
        s_step(c)
        return 0

    lax.fori_loop(nc - LEAD + 1, nc, rest_s, 0)

    def rest_f(c, _):
        f_step(c)
        return 0

    lax.fori_loop(nc - LEAD - 2, nc, rest_f, 0)

    inverse = lax.rsqrt(jnp.sum(acc1[...], axis=1, keepdims=True) / cols + EPS)
    factor = inverse * inverse * inverse * (jnp.sum(acc2[...], axis=1, keepdims=True) / cols)
    acc1[...] = jnp.broadcast_to(inverse, acc1.shape)
    acc2[...] = jnp.broadcast_to(factor, acc2.shape)

    def u_step(c, _):
        sc = scaled(c)
        for k in range(CW // 128):
            lane = slice(k * 128, (k + 1) * 128)
            ub[c, 0:tok, lane] = (acc1[...] * sc[:, lane] - sv[c, :, lane] * acc2[...]).astype(BF16)
        send_unit(c).start()
        return 0

    lax.fori_loop(0, nc, u_step, 0)
    wv[...] = jnp.full(wv.shape, 0.5 * weight, F32)
    send_weight.start()

    def d_step(c):
        def block(zd):
            at = at_rows(zd * rows, rows)
            pb[c, at, :] = dot(ht[at, :], ub[c]).astype(BF16)

        block(zo)
        for d in range(2):
            send_far(d, c).start()

        def others(j, _):
            block((z + j) % zs)
            return 0

        lax.fori_loop(0, 2, others, 0)
        block(zm)

    def b_step(c):
        for d in range(2):
            send_far(d, c).wait_recv()
            at = at_rows((zm if d else zp) * rows + d * half, half)
            pb[c, at, :] = (pb[c, at, :].astype(F32) + st1[d, c].astype(F32)).astype(BF16)
            send_near(d, c).start()

    def c_step(c):
        for d in range(2):
            send_near(d, c).wait_recv()
        total = pb[c, at_rows(z * rows, rows), :].astype(F32) + st2[0, c].astype(F32) + st2[1, c].astype(F32)
        ob[c] = (0.5 * (pv[c] - 0.004 * total)).astype(BF16)
        send_out(c).start()
        dwv[c] = total.astype(BF16)
        store_dw(c).start()

    gacc[...] = jnp.zeros_like(gacc)

    def g_step(c, _):
        send_unit(c).wait_recv()

        def part(t, _):
            at = at_rows(t * tok, tok)
            gacc[at, :] += dot_t(ub[c, at, :], wb[c])
            return 0

        lax.fori_loop(0, 2, part, 0)
        return 0

    def g_count(i):
        return jnp.minimum((5 * i + 2) // 4, nc)

    g_last = next(i for i in range(nc) if (5 * (i + 1) + 2) // 4 >= nc)

    def back_body(i, _):
        lax.fori_loop(g_count(i), g_count(i + 1), g_step, 0)

        @pl.when(i == g_last)
        def _():
            def give(p, _):
                here = at_rows(p * piece, piece)
                gsend[here, :] = gacc[at_rows(tok + p * piece, piece), :].astype(BF16)
                send_grad(p).start()
                return 0

            lax.fori_loop(0, PIECES, give, 0)
            gb[...] = gacc[0:tok, :].astype(BF16)
            store_own.start()

        d_step(i)

        @pl.when(i >= 1)
        def _():
            b_step(i - 1)

        @pl.when(i >= 2)
        def _():
            c_step(i - 2)

        return 0

    lax.fori_loop(0, nc, back_body, 0)
    b_step(nc - 1)
    c_step(nc - 2)
    c_step(nc - 1)

    def drain(c, _):
        for d in range(2):
            send_own(d, c).wait_send()
            send_on(d, c).wait_send()
            send_far(d, c).wait_send()
            send_near(d, c).wait_send()
        send_sum(c).wait_send()
        send_unit(c).wait_send()
        store_dw(c).wait()
        send_out(c).wait()
        return 0

    lax.fori_loop(0, nc, drain, 0)
    for p in range(PIECES):
        send_heads(p).wait_send()
        send_grad(p).wait()
    send_weight.wait()
    store_own.wait()


def step(by, params, push, heads, residual, cotangent, gain):
    rows, cols = params.shape
    tok = heads.shape[0]
    zs = lax.axis_size("fsdp") // 2
    nc = cols // CW
    kh = zs * rows
    half = rows // 2
    anywhere = pl.BlockSpec(memory_space=pl.ANY)
    dma = pltpu.SemaphoreType.DMA
    return pl.pallas_call(
        functools.partial(step_kernel, by, zs, heads.shape[1]),
        out_shape=(
            jax.ShapeDtypeStruct((tok, kh), BF16),
            jax.ShapeDtypeStruct((tok, kh), BF16),
            jax.ShapeDtypeStruct((rows, cols), BF16),
            jax.ShapeDtypeStruct((rows, cols), BF16),
            jax.ShapeDtypeStruct((8, 128), F32),
        ),
        in_specs=[
            anywhere,
            pl.BlockSpec(memory_space=pltpu.SMEM),
            anywhere,
            anywhere,
            anywhere,
            pl.BlockSpec(memory_space=pltpu.VMEM),
        ],
        out_specs=[anywhere] * 5,
        scratch_shapes=[
            pltpu.VMEM((nc, rows, CW), F32),
            pltpu.VMEM((tok, cols), BF16),
            pltpu.VMEM((tok, cols), BF16),
            pltpu.VMEM((tok, cols), BF16),
            pltpu.VMEM((2 * tok, kh), BF16),
            pltpu.VMEM((tok, kh), BF16),
            pltpu.VMEM((kh, 2 * tok), BF16),
            pltpu.VMEM((nc, kh, CW), BF16),
            pltpu.VMEM((nc, tok, CW), F32),
            pltpu.VMEM((nc, tok, CW), BF16),
            pltpu.VMEM((nc, tok, CW), BF16),
            pltpu.VMEM((tok, 128), F32),
            pltpu.VMEM((tok, 128), F32),
            pltpu.VMEM((nc, 2 * tok, CW), BF16),
            pltpu.VMEM((nc, kh, CW), BF16),
            pltpu.VMEM((2, nc, half, CW), BF16),
            pltpu.VMEM((2, nc, rows, CW), BF16),
            pltpu.VMEM((2 * tok, kh), F32),
            pltpu.VMEM((tok, kh), BF16),
            pltpu.VMEM((tok, kh), BF16),
            pltpu.VMEM((nc, rows, CW), BF16),
            pltpu.VMEM((nc, rows, CW), BF16),
            pltpu.VMEM((8, 128), F32),
            dma((nc,)), dma((3,)),
            dma((PIECES,)), dma((PIECES,)),
            dma((2, nc)), dma((2, nc)),
            dma((2, nc)), dma((2, nc)),
            dma((nc,)), dma((nc,)),
            dma((nc,)), dma((nc,)),
            dma((2, nc)), dma((2, nc)),
            dma((2, nc)), dma((2, nc)),
            dma((PIECES,)), dma((PIECES,)),
            dma((nc,)), dma((nc,)),
            dma((1,)), dma((1,)),
            dma((nc,)), dma((1,)),
        ],
        compiler_params=pltpu.CompilerParams(
            collective_id=by.bit_length(), has_side_effects=True, vmem_limit_bytes=62 * 2**20
        ),
        cost_estimate=pl.CostEstimate(
            flops=6 * tok * cols * heads.shape[1], bytes_accessed=20 * 2**20, transcendentals=tok
        ),
        name=f"push_sum_step_{by}",
    )(params, push, heads, residual, cotangent, gain)


def finish_kernel(zs, g_own, g_got, dw, box, params, inbox, grad, new, out):
    xl = lax.axis_index("fsdp") % 2
    width = g_own.shape[1] // zs
    for side_x in range(2):

        @pl.when(xl == side_x)
        def _():
            for s in range(2 * zs):
                src = g_own if s % 2 == side_x else g_got
                at = (s // 2) * width
                grad[:, s * width : (s + 1) * width] = src[:, at : at + width]

    new[...] = 0.5 * (params[...] - 0.004 * dw[...].astype(F32)) + inbox[...]
    out[...] = box[...].astype(F32)


def finish(g_own, g_got, dw, box, params, inbox):
    rows, cols = params.shape
    tok, kh = g_own.shape
    zs = lax.axis_size("fsdp") // 2
    steps = 4
    short = pl.BlockSpec((tok // steps, kh), lambda i: (i, 0))
    wide = pl.BlockSpec((tok // steps, 2 * kh), lambda i: (i, 0))
    block = pl.BlockSpec((rows // steps, cols), lambda i: (i, 0))
    return pl.pallas_call(
        functools.partial(finish_kernel, zs),
        grid=(steps,),
        out_shape=(
            jax.ShapeDtypeStruct((tok, 2 * kh), BF16),
            jax.ShapeDtypeStruct((rows, cols), F32),
            jax.ShapeDtypeStruct((rows, cols), F32),
        ),
        in_specs=[short, short, block, block, block, block],
        out_specs=[wide, block, block],
        compiler_params=pltpu.CompilerParams(vmem_limit_bytes=40 * 2**20),
        name="finish",
    )(g_own, g_got, dw, box, params, inbox)


def local(params, push_weight, inbox_params, inbox_weight, heads, residual, cotangent, gain, offset):
    levels = lax.axis_size("rep").bit_length() - 1
    powers = jnp.left_shift(jnp.ones((levels,), jnp.int32), jnp.arange(levels, dtype=jnp.int32))
    level = jnp.sum(jnp.where(powers == offset[0], jnp.arange(levels, dtype=jnp.int32), 0))
    operands = (params[0], push_weight, heads[0], residual[0], cotangent[0], gain[None])
    branches = [functools.partial(step, 1 << level_bit) for level_bit in range(levels)]
    g_own, g_got, dw, box, weight = lax.switch(level, branches, *operands)
    grad, new, out = finish(g_own, g_got, dw, box, params[0], inbox_params[0])
    return (new[None], 0.5 * push_weight + inbox_weight, out[None], weight[0, :1], grad[None])


def solution(mesh):
    block = P("rep", "fsdp", None)
    return jax.shard_map(
        local,
        mesh=mesh,
        in_specs=(block, P("rep"), block, P("rep"), block, block, block, P(), P()),
        out_specs=(block, P("rep"), block, P("rep"), block),
        check_vma=False,
    )
```

```python
import functools

import jax
import jax.numpy as jnp
from jax import lax
from jax.experimental import pallas as pl
from jax.experimental.pallas import tpu as pltpu
from jax.sharding import PartitionSpec as P

MESH = pl.DeviceIdType.MESH
F32 = jnp.float32
BF16 = jnp.bfloat16

CW = 256
LEAD = 4
EPS = 1e-05
VMEM_MB = 47


def dot(a, b):
    return jnp.dot(a, b, preferred_element_type=F32)


def dot_t(a, b):
    return lax.dot_general(a, b, (((1,), (1,)), ((), ())), preferred_element_type=F32)


def far_rows(by, rows):
    return {1: rows // 4, 2: 0}.get(by, rows // 2)


def step_kernel(
    by, inner,
    params, push, inbox, heads, residual, cotangent, gain,
    grad, new, outbox, w_out,
    pv, iv, rv, cv, gv, pw, hp, ht, wb, sv, sb, srv, acc1, acc2, ub, pb, st1, st2, wv,
    lp, lx, hs, hr, aos, aor, afs, afr, ss, sr, us, ur, s1s, s1r, s2s, s2r, gs, gr, os_, or_, ws, wr, nws, gos,
):
    rows, cols = params.shape
    tok = heads.shape[0]
    th = tok // 2
    nc = cols // CW
    kh = 4 * rows
    reps = lax.axis_size("rep")
    r = lax.axis_index("rep")
    f = lax.axis_index("fsdp")
    z, xl = f // 2, f % 2
    t = ((z + 1) // 2) % 2
    slot = (z // 2) * 2 + xl
    slots = ((z // 2) * 2 + 1 - xl, (1 - z // 2) * 2 + xl)
    far = 3 - slot
    ways = ((r, z * 2 + 1 - xl), (r, (3 - z) * 2 + xl))
    pair = (r, (z + 1 - 2 * (z % 2)) * 2 + xl)
    ahead, behind = ((r + by) % reps, f), ((r + reps - by) % reps, f)
    n0 = far_rows(by, rows)
    far_at, far_n = (0, n0), (n0, rows - n0)
    far_ways = [d for d in range(2) if far_n[d]]
    wide = 2 * rows
    mine = (t * wide, 3 * wide - t * wide)
    other = ((1 - t) * wide, 3 * wide - (1 - t) * wide)

    def remote(src, dst, send, recv, to):
        return pltpu.make_async_remote_copy(
            src_ref=src, dst_ref=dst, send_sem=send, recv_sem=recv, device_id=to, device_id_type=MESH
        )

    def at_cols(c):
        return pl.ds(pl.multiple_of(c * CW, CW), CW)

    def at_lanes(start, size):
        return pl.ds(pl.multiple_of(start, 128), size)

    def at_rows(start, size):
        return pl.ds(pl.multiple_of(start, 16), size)

    def load_params(c):
        return pltpu.make_async_copy(params.at[:, at_cols(c)], pv.at[c], lp.at[c])

    def load_heads(j):
        return pltpu.make_async_copy(
            heads.at[:, at_lanes(mine[j], wide)], hp.at[pl.ds(0, tok), pl.ds(j * wide, wide)], lx.at[j]
        )

    load_res = pltpu.make_async_copy(residual, rv, lx.at[2])
    load_cot = pltpu.make_async_copy(cotangent, cv, lx.at[3])
    load_gain = pltpu.make_async_copy(gain, gv, lx.at[4])
    load_inbox = pltpu.make_async_copy(inbox, iv, lx.at[5])
    load_push = pltpu.make_async_copy(push, pw, lx.at[6])

    def send_heads(h, j):
        return remote(
            heads.at[pl.ds(h * th, th), at_lanes(other[j], wide)],
            hp.at[pl.ds(tok + h * th, th), pl.ds(j * wide, wide)],
            hs.at[h, j], hr.at[h, j], pair,
        )

    def send_own(d, c):
        block = wb.at[c, at_rows(slot * rows, rows)]
        return remote(block, block, aos.at[d, c], aor.at[d, c], ways[d])

    def send_on(d, c):
        block = wb.at[c, at_rows(slots[1 - d] * rows + d * (rows // 2), rows // 2)]
        return remote(block, block, afs.at[d, c], afr.at[d, c], ways[d])

    def send_sum(c, h):
        return remote(sb.at[c, pl.ds(h * th, th)], srv.at[c, pl.ds(h * th, th)], ss.at[h, c], sr.at[h, c], pair)

    def send_unit(c, h):
        here, there = pl.ds(h * th, th), pl.ds(tok + h * th, th)
        return remote(ub.at[c, here], ub.at[c, there], us.at[h, c], ur.at[h, c], pair)

    def send_far(d, c):
        block = pb.at[c, at_rows(far * rows + far_at[d], far_n[d])]
        return remote(block, st1.at[c, pl.ds(far_at[d], far_n[d])], s1s.at[d, c], s1r.at[d, c], ways[d])

    def send_near(d, c):
        block = pb.at[c, at_rows(slots[d] * rows, rows)]
        return remote(block, st2.at[d, c], s2s.at[d, c], s2r.at[d, c], ways[d])

    def send_grad(h, j):
        here = pl.ds(h * th, th)
        return remote(
            hp.at[pl.ds(tok + h * th, th), pl.ds(j * wide, wide)], grad.at[here, at_lanes(mine[j], wide)],
            gs.at[h, j], gr.at[h, j], pair,
        )

    def send_out(c):
        return remote(pb.at[c, at_rows(slot * rows, rows)], outbox.at[:, at_cols(c)], os_.at[c], or_.at[c], ahead)

    send_weight = remote(wv, w_out, ws.at[0], wr.at[0], ahead)

    def store_new(c):
        return pltpu.make_async_copy(pv.at[c], new.at[:, at_cols(c)], nws.at[c])

    def store_grad(j):
        here = hp.at[pl.ds(0, tok), pl.ds(j * wide, wide)]
        return pltpu.make_async_copy(here, grad.at[:, at_lanes(mine[j], wide)], gos.at[j])

    load_push.start()
    for c in range(2):
        load_params(c).start()
    for j in range(2):
        load_heads(j).start()

    def loads(c, _):
        load_params(c).start()
        return 0

    lax.fori_loop(2, nc, loads, 0)
    load_gain.start()
    load_res.start()
    load_cot.start()
    load_inbox.start()

    barrier = pltpu.get_barrier_semaphore()
    for device in ways + (pair, ahead, behind):
        pl.semaphore_signal(barrier, inc=1, device_id=device, device_id_type=MESH)
    pl.semaphore_wait(barrier, 5)
    for h in range(2):
        for j in range(2):
            send_heads(h, j).start()

    load_push.wait()
    weight = pw[0]
    scale = (inner ** -0.5) / jnp.full((1, CW), weight, F32)

    def own_chunk(c):
        load_params(c).wait()
        wb[c, at_rows(slot * rows, rows), :] = (pv[c] * scale).astype(BF16)
        for d in range(2):
            send_own(d, c).start()

    def first_own(c, _):
        own_chunk(c)
        return 0

    lax.fori_loop(0, 2, first_own, 0)
    acc1[...] = jnp.zeros_like(acc1)
    acc2[...] = jnp.zeros_like(acc2)
    for j in range(2):
        load_heads(j).wait()
    load_gain.wait()
    load_res.wait()
    load_cot.wait()

    def z_step(c):
        @pl.when(c + 2 < nc)
        def _():
            own_chunk(c + 2)

        for d in range(2):
            send_own(d, c).wait_recv()
            send_on(1 - d, c).start()

    def s_ready(c):
        for d in range(2):
            send_on(d, c).wait_recv()

    def s_other(c, h):
        at = pl.ds(pl.multiple_of(h * th, th), th)
        sb[c, at, :] = dot(hp[pl.ds(pl.multiple_of(tok + h * th, th), th), :], wb[c]).astype(BF16)
        send_sum(c, h).start()

    def s_mine(c):
        sv[c] = dot(hp[0:tok, :], wb[c])

    def s_step(c, _):
        s_ready(c)

        def one(h, _):
            s_other(c, h)
            return 0

        lax.fori_loop(0, 2, one, 0)
        s_mine(c)
        return 0

    lanes = [slice(k * 128, (k + 1) * 128) for k in range(CW // 128)]

    def scaled(c, h):
        at = pl.ds(pl.multiple_of(h * th, th), th)
        cot = cv[at, at_cols(c)].astype(F32)
        return [gv[pl.ds(c * len(lanes) + k, 1), :] * cot[:, lane] for k, lane in enumerate(lanes)]

    def f_step(c, h):
        at = pl.ds(pl.multiple_of(h * th, th), th)
        send_sum(c, h).wait_recv()
        s = sv[c, at, :] + srv[c, at, :].astype(F32) + rv[at, at_cols(c)].astype(F32)
        sv[c, at, :] = s
        a1, a2 = acc1[at, :], acc2[at, :]
        for lane, sc in zip(lanes, scaled(c, h)):
            a1 += s[:, lane] * s[:, lane]
            a2 += sc * s[:, lane]
        acc1[at, :] = a1
        acc2[at, :] = a2

    def turn(j):
        ht[at_rows(j * 128, 128), :] = hp[:, at_lanes(j * 128, 128)].T

    def lead_body(i, _):
        z_step(i)
        return 0

    lax.fori_loop(0, LEAD - 1, lead_body, 0)
    s_ready(0)
    for h in range(2):
        for j in range(2):
            send_heads(h, j).wait_recv()
        s_other(0, h)
        if h == 0:
            z_step(LEAD - 1)
    s_mine(0)
    turns = kh // 128
    per = -(-turns // (nc - LEAD))
    twice = nc - 3

    def f_both(c, _):
        def one(h, _):
            f_step(c, h)
            return 0

        lax.fori_loop(0, 2, one, 0)
        return 0

    def main_body(i, _):
        z_step(i)
        late = (i > twice).astype(jnp.int32)
        both = (i >= twice).astype(jnp.int32)
        lax.fori_loop(i - LEAD + 1 + late, i - LEAD + 2 + both, s_step, 0)

        @pl.when(i >= LEAD + 2)
        def _():
            f_both(i - LEAD - 2, 0)

        def turn_body(j, _):
            turn(j)
            return 0

        first = (i - LEAD) * per
        lax.fori_loop(first, jnp.minimum(first + per, turns), turn_body, 0)
        return 0

    lax.fori_loop(LEAD, nc, main_body, 0)

    def last_sums(h, _):
        def one(c, _):
            @pl.when(h == 0)
            def _():
                s_ready(c)

            s_other(c, h)
            return 0

        lax.fori_loop(nc - 2, nc, one, 0)
        return 0

    lax.fori_loop(0, 2, last_sums, 0)
    for c in range(nc - 2, nc):
        s_mine(c)
    lax.fori_loop(nc - LEAD - 2, nc - 2, f_both, 0)

    def unit(c, h):
        at = pl.ds(pl.multiple_of(h * th, th), th)
        for lane, sc in zip(lanes, scaled(c, h)):
            ub[c, at, lane] = (acc1[at, :] * sc - sv[c, at, lane] * acc2[at, :]).astype(BF16)
        send_unit(c, h).start()

    def first_units(h, _):
        at = pl.ds(pl.multiple_of(h * th, th), th)

        def last_f(c, _):
            f_step(c, h)
            return 0

        lax.fori_loop(nc - 2, nc, last_f, 0)
        inverse = lax.rsqrt(jnp.sum(acc1[at, :], axis=1, keepdims=True) / cols + EPS)
        factor = inverse * inverse * inverse * (jnp.sum(acc2[at, :], axis=1, keepdims=True) / cols)
        acc1[at, :] = jnp.broadcast_to(inverse, (th, 128))
        acc2[at, :] = jnp.broadcast_to(factor, (th, 128))

        unit(0, h)
        return 0

    lax.fori_loop(0, 2, first_units, 0)

    def mid_units(c, _):
        def one(h, _):
            unit(c, h)
            return 0

        lax.fori_loop(0, 2, one, 0)
        return 0

    lax.fori_loop(1, nc - 2, mid_units, 0)

    def last_units(h, _):
        def one(c, _):
            unit(c, h)
            return 0

        lax.fori_loop(nc - 2, nc, one, 0)
        return 0

    lax.fori_loop(0, 2, last_units, 0)
    wv[...] = jnp.full(wv.shape, 0.5 * weight, F32)
    send_weight.start()
    load_inbox.wait()

    blocks = kh // CW

    def clear(k, _):
        sv[k] = jnp.zeros(sv.shape[1:], F32)
        return 0

    lax.fori_loop(0, 2 * blocks, clear, 0)

    def g_part(c, who, start, size):
        at = pl.ds(pl.multiple_of(start, th), size)
        part = dot_t(ub[c, pl.ds(pl.multiple_of(who * tok + start, th), size), :], wb[c])
        for k in range(blocks):
            sv[who * blocks + k, at, :] += part[:, k * CW : (k + 1) * CW]

    def g_half(c, h):
        send_unit(c, h).wait_recv()
        g_part(c, 1, h * th, th)

    def g_step(c, _):
        def one(h, _):
            g_half(c, h)
            return 0

        lax.fori_loop(0, 2, one, 0)
        g_part(c, 0, 0, tok)
        return 0

    def g_out(who, start, size):
        for k in range(blocks):
            part = sv[who * blocks + k, pl.ds(start, size), :].astype(BF16)
            hp[pl.ds(who * tok + start, size), k * CW : (k + 1) * CW] = part

    def g_last(h):
        for c in range(nc - 2, nc):
            g_half(c, h)
        g_out(1, h * th, th)
        for j in range(2):
            send_grad(h, j).start()

    def g_mine():
        for c in range(nc - 2, nc):
            g_part(c, 0, 0, tok)
        g_out(0, 0, tok)
        for j in range(2):
            store_grad(j).start()

    def g_count(i):
        return jnp.minimum(i + 1 + (i >= 3).astype(jnp.int32), nc - 2)

    def d_step(c):
        def block(s):
            at = at_rows(s * rows, rows)
            pb[c, at, :] = dot(ht[at, :], ub[c]).astype(BF16)

        block(far)
        for d in far_ways:
            send_far(d, c).start()

        def others(k, _):
            block((far + k) % 4)
            return 0

        lax.fori_loop(1, 4, others, 0)

    def b_step(c):
        for d in range(2):
            if d in far_ways:
                send_far(d, c).wait_recv()
                at = at_rows(slots[1 - d] * rows + far_at[d], far_n[d])
                got = st1[c, pl.ds(far_at[d], far_n[d]), :]
                pb[c, at, :] = (pb[c, at, :].astype(F32) + got.astype(F32)).astype(BF16)
            send_near(1 - d, c).start()

    def c_step(c):
        for d in range(2):
            send_near(d, c).wait_recv()
        total = pb[c, at_rows(slot * rows, rows), :].astype(F32) + st2[0, c].astype(F32) + st2[1, c].astype(F32)
        kept = 0.5 * (pv[c] - 0.004 * total)
        pb[c, at_rows(slot * rows, rows), :] = kept.astype(BF16)
        send_out(c).start()
        pv[c] = kept + iv[:, at_cols(c)]
        store_new(c).start()

    def back_body(i, _):
        before = jnp.where(i == 0, 0, g_count(i - 1))
        lax.fori_loop(before, g_count(i), g_step, 0)

        d_step(i)

        @pl.when(i >= 1)
        def _():
            b_step(i - 1)

        @pl.when(i == nc - 4)
        def _():
            g_last(0)

        @pl.when(i == nc - 3)
        def _():
            g_last(1)

        @pl.when(i >= 2)
        def _():
            c_step(i - 2)

        @pl.when(i == nc - 2)
        def _():
            g_mine()

        for d in range(2):
            send_own(d, i).wait_send()
            send_on(d, i).wait_send()
            send_sum(i, d).wait_send()
            send_unit(i, d).wait_send()
        return 0

    lax.fori_loop(0, nc, back_body, 0)
    b_step(nc - 1)
    c_step(nc - 2)
    c_step(nc - 1)

    def drain(c, _):
        for d in range(2):
            if d in far_ways:
                send_far(d, c).wait_send()
            send_near(d, c).wait_send()
        store_new(c).wait()
        send_out(c).wait()
        return 0

    lax.fori_loop(0, nc, drain, 0)
    for h in range(2):
        for j in range(2):
            send_heads(h, j).wait_send()
            send_grad(h, j).wait()
        store_grad(h).wait()
    send_weight.wait()


def step(by, params, push, inbox, heads, residual, cotangent, gain):
    rows, cols = params.shape
    tok = heads.shape[0]
    nc = cols // CW
    kh = 4 * rows
    anywhere = pl.BlockSpec(memory_space=pl.ANY)
    dma = pltpu.SemaphoreType.DMA
    return pl.pallas_call(
        functools.partial(step_kernel, by, heads.shape[1]),
        out_shape=(
            pltpu.VMEM(heads.shape, BF16),
            pltpu.VMEM((rows, cols), F32),
            pltpu.VMEM((rows, cols), BF16),
            pltpu.VMEM((8, 128), F32),
        ),
        in_specs=[pl.BlockSpec(memory_space=pltpu.HBM)] * 7,
        out_specs=[anywhere] * 4,
        scratch_shapes=[
            pltpu.VMEM((nc, rows, CW), F32),
            pltpu.VMEM((rows, cols), F32),
            pltpu.VMEM((tok, cols), BF16),
            pltpu.VMEM((tok, cols), BF16),
            pltpu.VMEM(gain.shape, F32),
            pltpu.SMEM((1,), F32),
            pltpu.VMEM((2 * tok, kh), BF16),
            pltpu.VMEM((kh, 2 * tok), BF16),
            pltpu.VMEM((nc, kh, CW), BF16),
            pltpu.VMEM((nc, tok, CW), F32),
            pltpu.VMEM((nc, tok, CW), BF16),
            pltpu.VMEM((nc, tok, CW), BF16),
            pltpu.VMEM((tok, 128), F32),
            pltpu.VMEM((tok, 128), F32),
            pltpu.VMEM((nc, 2 * tok, CW), BF16),
            pltpu.VMEM((nc, kh, CW), BF16),
            pltpu.VMEM((nc, rows, CW), BF16),
            pltpu.VMEM((2, nc, rows, CW), BF16),
            pltpu.VMEM((8, 128), F32),
            dma((nc,)), dma((7,)),
            dma((2, 2)), dma((2, 2)),
            dma((2, nc)), dma((2, nc)),
            dma((2, nc)), dma((2, nc)),
            dma((2, nc)), dma((2, nc)),
            dma((2, nc)), dma((2, nc)),
            dma((2, nc)), dma((2, nc)),
            dma((2, nc)), dma((2, nc)),
            dma((2, 2)), dma((2, 2)),
            dma((nc,)), dma((nc,)),
            dma((1,)), dma((1,)),
            dma((nc,)), dma((2,)),
        ],
        compiler_params=pltpu.CompilerParams(
            collective_id=by.bit_length(), has_side_effects=True, vmem_limit_bytes=VMEM_MB * 2**20
        ),
        cost_estimate=pl.CostEstimate(
            flops=6 * tok * cols * heads.shape[1], bytes_accessed=20 * 2**20, transcendentals=tok
        ),
        name=f"push_sum_step_{by}",
    )(params, push, inbox, heads, residual, cotangent, gain)


def finish_kernel(g_in, n_in, box, w_in, push, inbox, grad, new, out, w_out, w_new, ov, pw, iw, ww, sem, csem):
    ww[0] = w_in[0, 0]
    steps = sem.shape[0]
    size = box.shape[0] // steps
    copies = [
        pltpu.make_async_copy(push, pw, csem.at[0]),
        pltpu.make_async_copy(inbox, iw, csem.at[1]),
        pltpu.make_async_copy(n_in, new, csem.at[2]),
        pltpu.make_async_copy(g_in, grad, csem.at[3]),
        pltpu.make_async_copy(ww, w_out, csem.at[4]),
    ]
    for copy in copies:
        copy.start()
    for k in range(steps):
        at = pl.ds(k * size, size)
        ov[at, :] = box[at, :].astype(F32)
        copies.append(pltpu.make_async_copy(ov.at[at], out.at[at], sem.at[k]))
        copies[-1].start()
        if k == 0:
            copies[0].wait()
            copies[1].wait()
            pw[0] = 0.5 * pw[0] + iw[0]
            copies.append(pltpu.make_async_copy(pw, w_new, csem.at[5]))
            copies[-1].start()
    for copy in copies[2:]:
        copy.wait()


def finish(g_in, n_in, box, w_in, push, inbox):
    rows, cols = box.shape
    anywhere = pl.BlockSpec(memory_space=pl.ANY)
    steps = 4
    return pl.pallas_call(
        finish_kernel,
        out_shape=(
            jax.ShapeDtypeStruct(g_in.shape, BF16),
            jax.ShapeDtypeStruct((rows, cols), F32),
            jax.ShapeDtypeStruct((rows, cols), F32),
            jax.ShapeDtypeStruct((1,), F32),
            jax.ShapeDtypeStruct((1,), F32),
        ),
        in_specs=[pl.BlockSpec(memory_space=pltpu.VMEM)] * 4 + [pl.BlockSpec(memory_space=pltpu.HBM)] * 2,
        out_specs=[anywhere] * 5,
        scratch_shapes=[
            pltpu.VMEM((rows, cols), F32),
            pltpu.SMEM((1,), F32),
            pltpu.SMEM((1,), F32),
            pltpu.SMEM((1,), F32),
            pltpu.SemaphoreType.DMA((steps,)),
            pltpu.SemaphoreType.DMA((6,)),
        ],
        compiler_params=pltpu.CompilerParams(vmem_limit_bytes=16 * 2**20),
        name="finish",
    )(g_in, n_in, box, w_in, push, inbox)


def whole(by, params, push, inbox, inbox_weight, heads, residual, cotangent, gain):
    g, new, box, weight = step(by, params, push, inbox, heads, residual, cotangent, gain)
    return finish(g, new, box, weight, push, inbox_weight)


def local(params, push_weight, inbox_params, inbox_weight, heads, residual, cotangent, gain, offset):
    operands = (
        params[0], push_weight, inbox_params[0], inbox_weight, heads[0], residual[0], cotangent[0], gain.reshape(-1, 128)
    )
    branches = [functools.partial(whole, 1 << bit) for bit in range(4)]
    grad, new, out, weight, new_weight = lax.switch(offset[0] >> 1, branches, *operands)
    return (new[None], new_weight, out[None], weight, grad[None])


def solution(mesh):
    block = P("rep", "fsdp", None)
    return jax.shard_map(
        local,
        mesh=mesh,
        in_specs=(block, P("rep"), block, P("rep"), block, block, block, P(), P()),
        out_specs=(block, P("rep"), block, P("rep"), block),
        check_vma=False,
    )
```

```python
import functools

import jax
import jax.numpy as jnp
from jax import lax
from jax.experimental import pallas as pl
from jax.experimental.pallas import tpu as pltpu
from jax.sharding import PartitionSpec as P

MESH = pl.DeviceIdType.MESH
F32 = jnp.float32
BF16 = jnp.bfloat16

CW = 256
CF1, CF2 = 6, 2
LEAD = 4
AHEAD = 3
EPS = 1e-05
VMEM_MB = 51


def dot(a, b):
    return jnp.dot(a, b, preferred_element_type=F32)


def dot_t(a, b):
    return lax.dot_general(a, b, (((1,), (1,)), ((), ())), preferred_element_type=F32)


def loop(low, high, body):
    def run(i, _):
        body(i)
        return 0

    lax.fori_loop(low, high, run, 0)


def far_by_x(by, nc):
    return {1: CF1, 2: CF2}.get(by, nc)


def step_kernel(
    by, inner,
    params, push, inbox, heads, residual, cotangent, gain,
    grad, new, outbox, w_out,
    pv, iv, rv, cv, gv, pw, hp, ht, wb, sv, sb, srv, acc1, acc2, ub, pb, st1, st2, ga, wv,
    lp, lx, hs, hr, aos, aor, afs, afr, ss, sr, us, ur, s1s, s1r, s2s, s2r, gs, gr, os_, or_, ws, wr, nws, gos,
):
    rows, cols = params.shape
    tok = heads.shape[0]
    th = tok // 2
    nc = cols // CW
    kh = 4 * rows
    reps = lax.axis_size("rep")
    r = lax.axis_index("rep")
    f = lax.axis_index("fsdp")
    z, xl = f // 2, f % 2
    t = ((z + 1) // 2) % 2
    slot = (z // 2) * 2 + xl
    slots = ((z // 2) * 2 + 1 - xl, (1 - z // 2) * 2 + xl)
    far = 3 - slot
    ways = ((r, z * 2 + 1 - xl), (r, (3 - z) * 2 + xl))
    pair = (r, (z + 1 - 2 * (z % 2)) * 2 + xl)
    ahead, behind = ((r + by) % reps, f), ((r + reps - by) % reps, f)
    by_x = far_by_x(by, nc)
    half = rows // 2
    wide = 2 * rows
    mine = (t * wide, 3 * wide - t * wide)
    other = ((1 - t) * wide, 3 * wide - (1 - t) * wide)

    def remote(src, dst, send, recv, to):
        return pltpu.make_async_remote_copy(
            src_ref=src, dst_ref=dst, send_sem=send, recv_sem=recv, device_id=to, device_id_type=MESH
        )

    def at_cols(c):
        return pl.ds(pl.multiple_of(c * CW, CW), CW)

    def at_lanes(start, size):
        return pl.ds(pl.multiple_of(start, 128), size)

    def at_rows(start, size):
        return pl.ds(pl.multiple_of(start, 16), size)

    def load_params(c):
        return pltpu.make_async_copy(params.at[:, at_cols(c)], pv.at[c], lp.at[c])

    def load_heads(j):
        return pltpu.make_async_copy(
            heads.at[:, at_lanes(mine[j], wide)], hp.at[pl.ds(0, tok), pl.ds(j * wide, wide)], lx.at[j]
        )

    load_res = pltpu.make_async_copy(residual, rv, lx.at[2])
    load_cot = pltpu.make_async_copy(cotangent, cv, lx.at[3])
    load_gain = pltpu.make_async_copy(gain, gv, lx.at[4])
    load_inbox = pltpu.make_async_copy(inbox, iv, lx.at[5])
    load_push = pltpu.make_async_copy(push, pw, lx.at[6])

    def send_heads(h, j):
        return remote(
            heads.at[pl.ds(h * th, th), at_lanes(other[j], wide)],
            hp.at[pl.ds(tok + h * th, th), pl.ds(j * wide, wide)],
            hs.at[h, j], hr.at[h, j], pair,
        )

    def send_own(d, c):
        block = wb.at[c, at_rows(slot * rows, rows)]
        return remote(block, block, aos.at[d, c], aor.at[d, c], ways[d])

    def send_on(d, c):
        block = wb.at[c, at_rows(slots[1 - d] * rows + d * (rows // 2), rows // 2)]
        return remote(block, block, afs.at[d, c], afr.at[d, c], ways[d])

    def send_sum(c, h):
        return remote(sb.at[c, pl.ds(h * th, th)], srv.at[c, pl.ds(h * th, th)], ss.at[h, c], sr.at[h, c], pair)

    def send_unit(c, h):
        here, there = pl.ds(h * th, th), pl.ds(tok + h * th, th)
        return remote(ub.at[c, here], ub.at[c, there], us.at[h, c], ur.at[h, c], pair)

    def send_far(k, c):
        block = pb.at[c, at_rows(far * rows + k * half, half)]
        x_first = (c < by_x) & (k == 0)
        to = (r, jnp.where(x_first, ways[0][1], ways[1][1]))
        return remote(block, st1.at[c, pl.ds(k * half, half)], s1s.at[k, c], s1r.at[k, c], to)

    def send_near(d, c):
        block = pb.at[c, at_rows(slots[d] * rows, rows)]
        return remote(block, st2.at[d, c], s2s.at[d, c], s2r.at[d, c], ways[d])

    def send_grad(h, j):
        here = pl.ds(h * th, th)
        return remote(
            hp.at[pl.ds(tok + h * th, th), pl.ds(j * wide, wide)], grad.at[here, at_lanes(mine[j], wide)],
            gs.at[h, j], gr.at[h, j], pair,
        )

    def send_out(c):
        return remote(pb.at[c, at_rows(slot * rows, rows)], outbox.at[:, at_cols(c)], os_.at[c], or_.at[c], ahead)

    send_weight = remote(wv, w_out, ws.at[0], wr.at[0], ahead)

    def store_new(c):
        return pltpu.make_async_copy(pv.at[c], new.at[:, at_cols(c)], nws.at[c])

    def store_grad(j):
        here = hp.at[pl.ds(0, tok), pl.ds(j * wide, wide)]
        return pltpu.make_async_copy(here, grad.at[:, at_lanes(mine[j], wide)], gos.at[j])

    load_push.start()
    for c in range(2):
        load_params(c).start()
    for j in range(2):
        load_heads(j).start()

    loop(2, nc, lambda c: load_params(c).start())
    load_gain.start()
    load_res.start()
    load_cot.start()
    load_inbox.start()

    barrier = pltpu.get_barrier_semaphore()
    for device in ways + (pair, ahead, behind):
        pl.semaphore_signal(barrier, inc=1, device_id=device, device_id_type=MESH)
    pl.semaphore_wait(barrier, 5)
    for h in range(2):
        for j in range(2):
            send_heads(h, j).start()

    load_push.wait()
    weight = pw[0]
    scale = (inner ** -0.5) / jnp.full((1, CW), weight, F32)

    def own_chunk(c):
        load_params(c).wait()
        wb[c, at_rows(slot * rows, rows), :] = (pv[c] * scale).astype(BF16)
        for d in range(2):
            send_own(d, c).start()

    loop(0, 2, own_chunk)
    acc1[...] = jnp.zeros_like(acc1)
    acc2[...] = jnp.zeros_like(acc2)
    for j in range(2):
        load_heads(j).wait()
    load_gain.wait()
    load_res.wait()
    load_cot.wait()

    def z_step(c):
        @pl.when(c + 2 < nc)
        def _():
            own_chunk(c + 2)

        for d in range(2):
            send_own(d, c).wait_recv()
            send_on(1 - d, c).start()

    def s_ready(c):
        for d in range(2):
            send_on(d, c).wait_recv()

    def s_other(c, h):
        at = pl.ds(pl.multiple_of(h * th, th), th)
        sb[c, at, :] = dot(hp[pl.ds(pl.multiple_of(tok + h * th, th), th), :], wb[c]).astype(BF16)
        send_sum(c, h).start()

    def s_mine(c):
        sv[c] = dot(hp[0:tok, :], wb[c])

    def s_step(c):
        s_ready(c)
        loop(0, 2, lambda h: s_other(c, h))
        s_mine(c - 1)

    lanes = [slice(k * 128, (k + 1) * 128) for k in range(CW // 128)]

    def scaled(c, h):
        at = pl.ds(pl.multiple_of(h * th, th), th)
        cot = cv[at, at_cols(c)].astype(F32)
        return [gv[pl.ds(c * len(lanes) + k, 1), :] * cot[:, lane] for k, lane in enumerate(lanes)]

    def f_step(c, h):
        at = pl.ds(pl.multiple_of(h * th, th), th)
        send_sum(c, h).wait_recv()
        s = sv[c, at, :] + srv[c, at, :].astype(F32) + rv[at, at_cols(c)].astype(F32)
        sv[c, at, :] = s
        a1, a2 = acc1[at, :], acc2[at, :]
        for lane, sc in zip(lanes, scaled(c, h)):
            a1 += s[:, lane] * s[:, lane]
            a2 += sc * s[:, lane]
        acc1[at, :] = a1
        acc2[at, :] = a2

    def turn(j):
        ht[at_rows(j * 128, 128), :] = hp[:, at_lanes(j * 128, 128)].T

    def heads_in(h):
        for j in range(2):
            send_heads(h, j).wait_recv()

    def f_both(c):
        loop(0, 2, lambda h: f_step(c, h))

    loop(0, LEAD - 1, z_step)
    s_ready(0)
    turns = kh // 128
    per = -(-turns // (nc - LEAD))
    twice = nc - 3

    def main_body(i):
        @pl.when(i == LEAD - 1)
        def _():
            heads_in(0)
            s_other(0, 0)

        z_step(i)

        @pl.when(i == LEAD - 1)
        def _():
            heads_in(1)
            s_other(0, 1)

        @pl.when(i >= LEAD)
        def _():
            late = (i > twice).astype(jnp.int32)
            both = (i >= twice).astype(jnp.int32)
            loop(i - LEAD + 1 + late, i - LEAD + 2 + both, s_step)

            @pl.when(i >= LEAD + 2)
            def _():
                f_both(i - LEAD - 2)

            first = (i - LEAD) * per
            loop(first, jnp.minimum(first + per, turns), turn)

    blocks = kh // CW

    def clear(k):
        ga[k] = jnp.zeros(ga.shape[1:], F32)

    loop(0, 2 * blocks, clear)
    loop(LEAD - 1, nc, main_body)

    def last_sums(h):
        def one(c):
            @pl.when(h == 0)
            def _():
                s_ready(c)

            s_other(c, h)

        loop(nc - 2, nc, one)

    loop(0, 2, last_sums)
    loop(nc - 3, nc, s_mine)

    def unit(c, h):
        at = pl.ds(pl.multiple_of(h * th, th), th)
        for lane, sc in zip(lanes, scaled(c, h)):
            ub[c, at, lane] = (acc1[at, :] * sc - sv[c, at, lane] * acc2[at, :]).astype(BF16)
        send_unit(c, h).start()

    def first_units(h):
        at = pl.ds(pl.multiple_of(h * th, th), th)

        loop((nc - LEAD - 2) * 2 * (1 - h), (nc - 2) * 2 * (1 - h), lambda k: f_step(k // 2, k % 2))
        loop(nc - 2, nc, lambda c: f_step(c, h))
        inverse = lax.rsqrt(jnp.sum(acc1[at, :], axis=1, keepdims=True) / cols + EPS)
        factor = inverse * inverse * inverse * (jnp.sum(acc2[at, :], axis=1, keepdims=True) / cols)
        acc1[at, :] = jnp.broadcast_to(inverse, (th, 128))
        acc2[at, :] = jnp.broadcast_to(factor, (th, 128))
        unit(0, h)

    loop(0, 2, first_units)

    def units(k):
        c, h = k // 2, k % 2
        tail = (c >= nc - 2).astype(jnp.int32)
        j = k - 2 * (nc - 2)
        unit(c + tail * (nc - 2 + j % 2 - c), h + tail * (j // 2 - h))

    loop(2, 2 * AHEAD, units)
    wv[...] = jnp.full(wv.shape, 0.5 * weight, F32)
    send_weight.start()
    load_inbox.wait()

    def g_part(c, who, start, size):
        at = pl.ds(pl.multiple_of(start, th), size)
        add = dot_t(ub[c, pl.ds(pl.multiple_of(who * tok + start, th), size), :], wb[c])
        for k in range(blocks):
            ga[who * blocks + k, at, :] += add[:, k * CW : (k + 1) * CW]

    def g_out(who, start, size):
        at, to = pl.ds(pl.multiple_of(start, th), size), pl.ds(pl.multiple_of(who * tok + start, th), size)
        for k in range(blocks):
            hp[to, k * CW : (k + 1) * CW] = ga[who * blocks + k, at, :].astype(BF16)

    def g_count(i):
        return jnp.minimum(i + 1 + (i >= 3).astype(jnp.int32), nc - 2)

    def u_wait(c):
        for h in range(2):
            send_unit(c, h).wait_recv()

    def g_last(h):
        def one(c):
            send_unit(c, h).wait_recv()
            g_part(c, 1, h * th, th)

        loop(nc - 2, nc, one)
        g_out(1, h * th, th)
        for j in range(2):
            send_grad(h, j).start()

    def d_step(c):
        def block(s):
            at = at_rows(s * rows, rows)
            pb[c, at, :] = dot(ht[at, :], ub[c]).astype(BF16)

        def one(k):
            block((far + k) % 4)

            @pl.when(k == 0)
            def _():
                for d in range(2):
                    send_far(d, c).start()

        loop(0, 4, one)

    def b_step(c):
        for k in range(2):
            send_far(k, c).wait_recv()
            x_first = (c < by_x) & (k == 0)
            at = at_rows(jnp.where(x_first, slots[1], slots[0]) * rows + k * half, half)
            pb[c, at, :] = (pb[c, at, :].astype(F32) + st1[c, k * half : (k + 1) * half, :].astype(F32)).astype(BF16)
        for d in range(2):
            send_near(d, c).start()

    def c_step(c):
        for d in range(2):
            send_near(d, c).wait_recv()
        total = pb[c, at_rows(slot * rows, rows), :].astype(F32) + st2[0, c].astype(F32) + st2[1, c].astype(F32)
        kept = 0.5 * (pv[c] - 0.004 * total)
        pb[c, at_rows(slot * rows, rows), :] = kept.astype(BF16)
        send_out(c).start()
        pv[c] = kept + iv[:, at_cols(c)]
        store_new(c).start()

    def back_body(i):
        before, now = jnp.where(i == 0, 0, g_count(i - 1)), g_count(i)
        loop(before, now, u_wait)

        @pl.when(i < nc)
        def _():
            d_step(i)

        @pl.when((i >= 1) & (i <= nc))
        def _():
            b_step(i - 1)

        loop(jnp.minimum(2 * (AHEAD + 2 * i), 2 * nc), jnp.minimum(2 * (AHEAD + 2 * i + 2), 2 * nc), units)

        mine = (i == nc - 2).astype(jnp.int32)
        loop(
            before, now + 2 * mine, lambda c: loop(0, 2 - mine, lambda who: g_part(c, who, 0, tok))
        )

        @pl.when((i == nc - 4) | (i == nc - 3))
        def _():
            g_last(i - nc + 4)

        @pl.when(i >= 2)
        def _():
            c_step(i - 2)

        @pl.when(i == nc - 2)
        def _():
            g_out(0, 0, tok)
            for j in range(2):
                store_grad(j).start()

        @pl.when(i < nc)
        def _():
            for d in range(2):
                send_own(d, i).wait_send()
                send_on(d, i).wait_send()
                send_sum(i, d).wait_send()
                send_unit(i, d).wait_send()

    loop(0, nc + 2, back_body)

    def drain(c):
        for d in range(2):
            send_far(d, c).wait_send()
            send_near(d, c).wait_send()
        store_new(c).wait()
        send_out(c).wait()

    loop(0, nc, drain)
    for h in range(2):
        for j in range(2):
            send_heads(h, j).wait_send()
            send_grad(h, j).wait()
        store_grad(h).wait()
    send_weight.wait()


def step(by, params, push, inbox, heads, residual, cotangent, gain):
    rows, cols = params.shape
    tok = heads.shape[0]
    nc = cols // CW
    kh = 4 * rows
    anywhere = pl.BlockSpec(memory_space=pl.ANY)
    dma = pltpu.SemaphoreType.DMA
    return pl.pallas_call(
        functools.partial(step_kernel, by, heads.shape[1]),
        out_shape=(
            pltpu.VMEM(heads.shape, BF16),
            pltpu.VMEM((rows, cols), F32),
            pltpu.VMEM((rows, cols), BF16),
            pltpu.VMEM((8, 128), F32),
        ),
        in_specs=[pl.BlockSpec(memory_space=pltpu.HBM)] * 7,
        out_specs=[anywhere] * 4,
        scratch_shapes=[
            pltpu.VMEM((nc, rows, CW), F32),
            pltpu.VMEM((rows, cols), F32),
            pltpu.VMEM((tok, cols), BF16),
            pltpu.VMEM((tok, cols), BF16),
            pltpu.VMEM(gain.shape, F32),
            pltpu.SMEM((1,), F32),
            pltpu.VMEM((2 * tok, kh), BF16),
            pltpu.VMEM((kh, 2 * tok), BF16),
            pltpu.VMEM((nc, kh, CW), BF16),
            pltpu.VMEM((nc, tok, CW), F32),
            pltpu.VMEM((nc, tok, CW), BF16),
            pltpu.VMEM((nc, tok, CW), BF16),
            pltpu.VMEM((tok, 128), F32),
            pltpu.VMEM((tok, 128), F32),
            pltpu.VMEM((nc, 2 * tok, CW), BF16),
            pltpu.VMEM((nc, kh, CW), BF16),
            pltpu.VMEM((nc, rows, CW), BF16),
            pltpu.VMEM((2, nc, rows, CW), BF16),
            pltpu.VMEM((2 * kh // CW, tok, CW), F32),
            pltpu.VMEM((8, 128), F32),
            dma((nc,)), dma((7,)),
            dma((2, 2)), dma((2, 2)),
            dma((2, nc)), dma((2, nc)),
            dma((2, nc)), dma((2, nc)),
            dma((2, nc)), dma((2, nc)),
            dma((2, nc)), dma((2, nc)),
            dma((2, nc)), dma((2, nc)),
            dma((2, nc)), dma((2, nc)),
            dma((2, 2)), dma((2, 2)),
            dma((nc,)), dma((nc,)),
            dma((1,)), dma((1,)),
            dma((nc,)), dma((2,)),
        ],
        compiler_params=pltpu.CompilerParams(
            collective_id=by.bit_length(), has_side_effects=True, vmem_limit_bytes=VMEM_MB * 2**20
        ),
        cost_estimate=pl.CostEstimate(
            flops=6 * tok * cols * heads.shape[1], bytes_accessed=20 * 2**20, transcendentals=tok
        ),
        name=f"push_sum_step_{by}",
    )(params, push, inbox, heads, residual, cotangent, gain)


def finish_kernel(g_in, n_in, box, w_in, push, inbox, grad, new, out, w_out, w_new, ov, pw, iw, ww, sem, csem):
    ww[0] = w_in[0, 0]
    steps = sem.shape[0]
    size = box.shape[0] // steps
    copies = [
        pltpu.make_async_copy(push, pw, csem.at[0]),
        pltpu.make_async_copy(inbox, iw, csem.at[1]),
        pltpu.make_async_copy(n_in, new, csem.at[2]),
        pltpu.make_async_copy(g_in, grad, csem.at[3]),
        pltpu.make_async_copy(ww, w_out, csem.at[4]),
    ]
    for copy in copies:
        copy.start()
    for k in range(steps):
        at = pl.ds(k * size, size)
        ov[at, :] = box[at, :].astype(F32)
        copies.append(pltpu.make_async_copy(ov.at[at], out.at[at], sem.at[k]))
        copies[-1].start()
        if k == 0:
            copies[0].wait()
            copies[1].wait()
            pw[0] = 0.5 * pw[0] + iw[0]
            copies.append(pltpu.make_async_copy(pw, w_new, csem.at[5]))
            copies[-1].start()
    for copy in copies[2:]:
        copy.wait()


def finish(g_in, n_in, box, w_in, push, inbox):
    rows, cols = box.shape
    anywhere = pl.BlockSpec(memory_space=pl.ANY)
    steps = 4
    return pl.pallas_call(
        finish_kernel,
        out_shape=(
            jax.ShapeDtypeStruct(g_in.shape, BF16),
            jax.ShapeDtypeStruct((rows, cols), F32),
            jax.ShapeDtypeStruct((rows, cols), F32),
            jax.ShapeDtypeStruct((1,), F32),
            jax.ShapeDtypeStruct((1,), F32),
        ),
        in_specs=[pl.BlockSpec(memory_space=pltpu.VMEM)] * 4 + [pl.BlockSpec(memory_space=pltpu.HBM)] * 2,
        out_specs=[anywhere] * 5,
        scratch_shapes=[
            pltpu.VMEM((rows, cols), F32),
            pltpu.SMEM((1,), F32),
            pltpu.SMEM((1,), F32),
            pltpu.SMEM((1,), F32),
            pltpu.SemaphoreType.DMA((steps,)),
            pltpu.SemaphoreType.DMA((6,)),
        ],
        compiler_params=pltpu.CompilerParams(vmem_limit_bytes=16 * 2**20),
        name="finish",
    )(g_in, n_in, box, w_in, push, inbox)


def whole(by, params, push, inbox, inbox_weight, heads, residual, cotangent, gain):
    g, new, box, weight = step(by, params, push, inbox, heads, residual, cotangent, gain)
    return finish(g, new, box, weight, push, inbox_weight)


def local(params, push_weight, inbox_params, inbox_weight, heads, residual, cotangent, gain, offset):
    operands = (
        params[0], push_weight, inbox_params[0], inbox_weight, heads[0], residual[0], cotangent[0], gain.reshape(-1, 128)
    )
    branches = [functools.partial(whole, 1 << bit) for bit in range(4)]
    grad, new, out, weight, new_weight = lax.switch(offset[0] >> 1, branches, *operands)
    return (new[None], new_weight, out[None], weight, grad[None])


def solution(mesh):
    block = P("rep", "fsdp", None)
    return jax.shard_map(
        local,
        mesh=mesh,
        in_specs=(block, P("rep"), block, P("rep"), block, block, block, P(), P()),
        out_specs=(block, P("rep"), block, P("rep"), block),
        check_vma=False,
    )
```

```python
import functools

import jax
import jax.numpy as jnp
from jax import lax
from jax.experimental import pallas as pl
from jax.experimental.pallas import tpu as pltpu
from jax.sharding import PartitionSpec as P

MESH = pl.DeviceIdType.MESH
F32 = jnp.float32
BF16 = jnp.bfloat16

CW = 256
CF1, CF2 = 6, 2
LEAD = 4
AHEAD = 3
EPS = 1e-05
VMEM_MB = 51


def dot(a, b):
    return jnp.dot(a, b, preferred_element_type=F32)


def dot_t(a, b):
    return lax.dot_general(a, b, (((1,), (1,)), ((), ())), preferred_element_type=F32)


def loop(low, high, body):
    def run(i, _):
        body(i)
        return 0

    lax.fori_loop(low, high, run, 0)


def far_by_x(by, nc):
    return {1: CF1, 2: CF2}.get(by, nc)


def step_kernel(
    by, inner,
    params, push, inbox, heads, residual, cotangent, gain,
    grad, new, outbox, w_out,
    pv, iv, rv, cv, gv, pw, hp, ht, wb, sv, sb, srv, acc1, acc2, ub, pb, st1, st2, ga, wv,
    lp, lx, hs, hr, aos, aor, afs, afr, ss, sr, us, ur, s1s, s1r, s2s, s2r, gs, gr, os_, or_, ws, wr, nws, gos,
):
    rows, cols = params.shape
    tok = heads.shape[0]
    th = tok // 2
    nc = cols // CW
    kh = 4 * rows
    reps = lax.axis_size("rep")
    r = lax.axis_index("rep")
    f = lax.axis_index("fsdp")
    z, xl = f // 2, f % 2
    t = ((z + 1) // 2) % 2
    slot = (z // 2) * 2 + xl
    slots = ((z // 2) * 2 + 1 - xl, (1 - z // 2) * 2 + xl)
    far = 3 - slot
    ways = ((r, z * 2 + 1 - xl), (r, (3 - z) * 2 + xl))
    pair = (r, (z + 1 - 2 * (z % 2)) * 2 + xl)
    ahead, behind = ((r + by) % reps, f), ((r + reps - by) % reps, f)
    by_x = far_by_x(by, nc)
    half = rows // 2
    wide = 2 * rows
    mine = (t * wide, 3 * wide - t * wide)
    other = ((1 - t) * wide, 3 * wide - (1 - t) * wide)

    def remote(src, dst, send, recv, to):
        return pltpu.make_async_remote_copy(
            src_ref=src, dst_ref=dst, send_sem=send, recv_sem=recv, device_id=to, device_id_type=MESH
        )

    def at_cols(c):
        return pl.ds(pl.multiple_of(c * CW, CW), CW)

    def at_lanes(start, size):
        return pl.ds(pl.multiple_of(start, 128), size)

    def at_rows(start, size):
        return pl.ds(pl.multiple_of(start, 16), size)

    def load_params(c):
        return pltpu.make_async_copy(params.at[:, at_cols(c)], pv.at[c], lp.at[c])

    def load_heads(j):
        return pltpu.make_async_copy(
            heads.at[:, at_lanes(mine[j], wide)], hp.at[pl.ds(0, tok), pl.ds(j * wide, wide)], lx.at[j]
        )

    load_res = pltpu.make_async_copy(residual, rv, lx.at[2])
    load_cot = pltpu.make_async_copy(cotangent, cv, lx.at[3])
    load_gain = pltpu.make_async_copy(gain, gv, lx.at[4])
    load_inbox = pltpu.make_async_copy(inbox, iv, lx.at[5])
    load_push = pltpu.make_async_copy(push, pw, lx.at[6])

    def send_heads(h, j):
        return remote(
            heads.at[pl.ds(h * th, th), at_lanes(other[j], wide)],
            hp.at[pl.ds(tok + h * th, th), pl.ds(j * wide, wide)],
            hs.at[h, j], hr.at[h, j], pair,
        )

    def send_own(d, c):
        block = wb.at[c, at_rows(slot * rows, rows)]
        return remote(block, block, aos.at[d, c], aor.at[d, c], ways[d])

    def send_on(d, c):
        block = wb.at[c, at_rows(slots[1 - d] * rows + d * (rows // 2), rows // 2)]
        return remote(block, block, afs.at[d, c], afr.at[d, c], ways[d])

    def send_sum(c, h):
        return remote(sb.at[c, pl.ds(h * th, th)], srv.at[c, pl.ds(h * th, th)], ss.at[h, c], sr.at[h, c], pair)

    def send_unit(c, h):
        here, there = pl.ds(h * th, th), pl.ds(tok + h * th, th)
        return remote(ub.at[c, here], ub.at[c, there], us.at[h, c], ur.at[h, c], pair)

    end = nc - 1

    def part_lanes(part):
        return at_lanes(part * (CW // 2), CW // 2)

    def part_cols(part):
        return at_lanes(end * CW + part * (CW // 2), CW // 2)

    def part_far(k, part):
        lanes, q = part_lanes(part), end + part
        block = pb.at[end, at_rows(far * rows + k * half, half), lanes]
        to = ways[0] if k == 0 and end < by_x else ways[1]
        return remote(block, st1.at[end, pl.ds(k * half, half), lanes], s1s.at[k, q], s1r.at[k, q], to)

    def part_near(d, part):
        lanes, q = part_lanes(part), end + part
        block = pb.at[end, at_rows(slots[d] * rows, rows), lanes]
        return remote(block, st2.at[d, end, :, lanes], s2s.at[d, q], s2r.at[d, q], ways[d])

    def part_out(part):
        block = pb.at[end, at_rows(slot * rows, rows), part_lanes(part)]
        return remote(block, outbox.at[:, part_cols(part)], os_.at[end + part], or_.at[end + part], ahead)

    def part_new(part):
        return pltpu.make_async_copy(pv.at[end, :, part_lanes(part)], new.at[:, part_cols(part)], nws.at[end + part])

    def send_far(k, c):
        block = pb.at[c, at_rows(far * rows + k * half, half)]
        x_first = (c < by_x) & (k == 0)
        to = (r, jnp.where(x_first, ways[0][1], ways[1][1]))
        return remote(block, st1.at[c, pl.ds(k * half, half)], s1s.at[k, c], s1r.at[k, c], to)

    def send_near(d, c):
        block = pb.at[c, at_rows(slots[d] * rows, rows)]
        return remote(block, st2.at[d, c], s2s.at[d, c], s2r.at[d, c], ways[d])

    def send_grad(h, j):
        here = pl.ds(h * th, th)
        return remote(
            hp.at[pl.ds(tok + h * th, th), pl.ds(j * wide, wide)], grad.at[here, at_lanes(mine[j], wide)],
            gs.at[h, j], gr.at[h, j], pair,
        )

    def send_out(c):
        return remote(pb.at[c, at_rows(slot * rows, rows)], outbox.at[:, at_cols(c)], os_.at[c], or_.at[c], ahead)

    send_weight = remote(wv, w_out, ws.at[0], wr.at[0], ahead)

    def store_new(c):
        return pltpu.make_async_copy(pv.at[c], new.at[:, at_cols(c)], nws.at[c])

    def store_grad(j):
        here = hp.at[pl.ds(0, tok), pl.ds(j * wide, wide)]
        return pltpu.make_async_copy(here, grad.at[:, at_lanes(mine[j], wide)], gos.at[j])

    load_push.start()
    for c in range(2):
        load_params(c).start()
    for j in range(2):
        load_heads(j).start()

    loop(2, nc, lambda c: load_params(c).start())
    load_gain.start()
    load_res.start()
    load_cot.start()
    load_inbox.start()

    barrier = pltpu.get_barrier_semaphore()
    for device in ways + (pair, ahead, behind):
        pl.semaphore_signal(barrier, inc=1, device_id=device, device_id_type=MESH)
    pl.semaphore_wait(barrier, 5)
    for h in range(2):
        for j in range(2):
            send_heads(h, j).start()

    load_push.wait()
    weight = pw[0]
    scale = (inner ** -0.5) / jnp.full((1, CW), weight, F32)

    def own_chunk(c):
        load_params(c).wait()
        wb[c, at_rows(slot * rows, rows), :] = (pv[c] * scale).astype(BF16)
        for d in range(2):
            send_own(d, c).start()

    loop(0, 2, own_chunk)
    acc1[...] = jnp.zeros_like(acc1)
    acc2[...] = jnp.zeros_like(acc2)
    for j in range(2):
        load_heads(j).wait()
    load_gain.wait()
    load_res.wait()
    load_cot.wait()

    def z_step(c):
        @pl.when(c + 2 < nc)
        def _():
            own_chunk(c + 2)

        for d in range(2):
            send_own(d, c).wait_recv()
            send_on(1 - d, c).start()

    def s_ready(c):
        for d in range(2):
            send_on(d, c).wait_recv()

    def s_other(c, h):
        at = pl.ds(pl.multiple_of(h * th, th), th)
        sb[c, at, :] = dot(hp[pl.ds(pl.multiple_of(tok + h * th, th), th), :], wb[c]).astype(BF16)
        send_sum(c, h).start()

    def s_mine(c):
        sv[c] = dot(hp[0:tok, :], wb[c])

    def s_step(c):
        s_ready(c)
        loop(0, 2, lambda h: s_other(c, h))
        s_mine(c - 1)

    lanes = [slice(k * 128, (k + 1) * 128) for k in range(CW // 128)]

    def scaled(c, h):
        at = pl.ds(pl.multiple_of(h * th, th), th)
        cot = cv[at, at_cols(c)].astype(F32)
        return [gv[pl.ds(c * len(lanes) + k, 1), :] * cot[:, lane] for k, lane in enumerate(lanes)]

    def f_step(c, h):
        at = pl.ds(pl.multiple_of(h * th, th), th)
        send_sum(c, h).wait_recv()
        s = sv[c, at, :] + srv[c, at, :].astype(F32) + rv[at, at_cols(c)].astype(F32)
        sv[c, at, :] = s
        a1, a2 = acc1[at, :], acc2[at, :]
        for lane, sc in zip(lanes, scaled(c, h)):
            a1 += s[:, lane] * s[:, lane]
            a2 += sc * s[:, lane]
        acc1[at, :] = a1
        acc2[at, :] = a2

    def turn(j):
        ht[at_rows(j * 128, 128), :] = hp[:, at_lanes(j * 128, 128)].T

    def heads_in(h):
        for j in range(2):
            send_heads(h, j).wait_recv()

    def f_both(c):
        loop(0, 2, lambda h: f_step(c, h))

    loop(0, LEAD - 1, z_step)
    s_ready(0)
    turns = kh // 128
    per = -(-turns // (nc - LEAD))
    twice = nc - 3

    def main_body(i):
        @pl.when(i == LEAD - 1)
        def _():
            heads_in(0)
            s_other(0, 0)

        z_step(i)

        @pl.when(i == LEAD - 1)
        def _():
            heads_in(1)
            s_other(0, 1)

        @pl.when(i >= LEAD)
        def _():
            late = (i > twice).astype(jnp.int32)
            both = (i >= twice).astype(jnp.int32)
            loop(i - LEAD + 1 + late, i - LEAD + 2 + both, s_step)

            @pl.when(i >= LEAD + 2)
            def _():
                f_both(i - LEAD - 2)

            first = (i - LEAD) * per
            loop(first, jnp.minimum(first + per, turns), turn)

    blocks = kh // CW

    def clear(k):
        ga[k] = jnp.zeros(ga.shape[1:], F32)

    loop(0, 2 * blocks, clear)
    loop(LEAD - 1, nc, main_body)

    def last_sums(h):
        def one(c):
            @pl.when(h == 0)
            def _():
                s_ready(c)

            s_other(c, h)

        loop(nc - 2, nc, one)

    loop(0, 2, last_sums)
    loop(nc - 3, nc, s_mine)

    def unit(c, h):
        at = pl.ds(pl.multiple_of(h * th, th), th)
        for lane, sc in zip(lanes, scaled(c, h)):
            ub[c, at, lane] = (acc1[at, :] * sc - sv[c, at, lane] * acc2[at, :]).astype(BF16)
        send_unit(c, h).start()

    def first_units(h):
        at = pl.ds(pl.multiple_of(h * th, th), th)

        loop((nc - LEAD - 2) * 2 * (1 - h), (nc - 2) * 2 * (1 - h), lambda k: f_step(k // 2, k % 2))
        loop(nc - 2, nc, lambda c: f_step(c, h))
        inverse = lax.rsqrt(jnp.sum(acc1[at, :], axis=1, keepdims=True) / cols + EPS)
        factor = inverse * inverse * inverse * (jnp.sum(acc2[at, :], axis=1, keepdims=True) / cols)
        acc1[at, :] = jnp.broadcast_to(inverse, (th, 128))
        acc2[at, :] = jnp.broadcast_to(factor, (th, 128))
        unit(0, h)

    loop(0, 2, first_units)

    def units(k):
        c, h = k // 2, k % 2
        tail = (c >= nc - 2).astype(jnp.int32)
        j = k - 2 * (nc - 2)
        unit(c + tail * (nc - 2 + j % 2 - c), h + tail * (j // 2 - h))

    loop(2, 2 * AHEAD, units)
    wv[...] = jnp.full(wv.shape, 0.5 * weight, F32)
    send_weight.start()
    load_inbox.wait()

    def g_part(c, who, start, size):
        at = pl.ds(pl.multiple_of(start, th), size)
        add = dot_t(ub[c, pl.ds(pl.multiple_of(who * tok + start, th), size), :], wb[c])
        for k in range(blocks):
            ga[who * blocks + k, at, :] += add[:, k * CW : (k + 1) * CW]

    def g_out(who, start, size):
        at, to = pl.ds(pl.multiple_of(start, th), size), pl.ds(pl.multiple_of(who * tok + start, th), size)
        for k in range(blocks):
            hp[to, k * CW : (k + 1) * CW] = ga[who * blocks + k, at, :].astype(BF16)

    def g_count(i):
        return jnp.minimum(i + 1 + (i >= 3).astype(jnp.int32), nc - 2)

    def u_wait(c):
        for h in range(2):
            send_unit(c, h).wait_recv()

    def g_last(h):
        def one(c):
            send_unit(c, h).wait_recv()
            g_part(c, 1, h * th, th)

        loop(nc - 2, nc, one)
        g_out(1, h * th, th)
        for j in range(2):
            send_grad(h, j).start()

    def d_step(c):
        def block(s):
            at = at_rows(s * rows, rows)
            pb[c, at, :] = dot(ht[at, :], ub[c]).astype(BF16)

        def one(k):
            block((far + k) % 4)

            @pl.when((k == 0) & (c < end))
            def _():
                for d in range(2):
                    send_far(d, c).start()

            @pl.when((k == 0) & (c == end))
            def _():
                for part in range(2):
                    for d in range(2):
                        part_far(d, part).start()

        loop(0, 4, one)

    def b_step(c):
        for k in range(2):
            send_far(k, c).wait_recv()
            x_first = (c < by_x) & (k == 0)
            at = at_rows(jnp.where(x_first, slots[1], slots[0]) * rows + k * half, half)
            pb[c, at, :] = (pb[c, at, :].astype(F32) + st1[c, k * half : (k + 1) * half, :].astype(F32)).astype(BF16)
        for d in range(2):
            send_near(d, c).start()

    def b_part(part):
        lanes = part_lanes(part)
        for k in range(2):
            part_far(k, part).wait_recv()
            at = at_rows((slots[1] if k == 0 and end < by_x else slots[0]) * rows + k * half, half)
            got = st1[end, k * half : (k + 1) * half, lanes]
            pb[end, at, lanes] = (pb[end, at, lanes].astype(F32) + got.astype(F32)).astype(BF16)
        for d in range(2):
            part_near(d, part).start()

    def c_part(part):
        lanes, at = part_lanes(part), at_rows(slot * rows, rows)
        for d in range(2):
            part_near(d, part).wait_recv()
        total = pb[end, at, lanes].astype(F32) + st2[0, end, :, lanes].astype(F32) + st2[1, end, :, lanes].astype(F32)
        kept = 0.5 * (pv[end, :, lanes] - 0.004 * total)
        pb[end, at, lanes] = kept.astype(BF16)
        part_out(part).start()
        pv[end, :, lanes] = kept + iv[:, part_cols(part)]
        part_new(part).start()

    def c_step(c):
        for d in range(2):
            send_near(d, c).wait_recv()
        total = pb[c, at_rows(slot * rows, rows), :].astype(F32) + st2[0, c].astype(F32) + st2[1, c].astype(F32)
        kept = 0.5 * (pv[c] - 0.004 * total)
        pb[c, at_rows(slot * rows, rows), :] = kept.astype(BF16)
        send_out(c).start()
        pv[c] = kept + iv[:, at_cols(c)]
        store_new(c).start()

    def back_body(i):
        before, now = jnp.where(i == 0, 0, g_count(i - 1)), g_count(i)
        loop(before, now, u_wait)

        @pl.when(i < nc)
        def _():
            d_step(i)

        @pl.when((i >= 1) & (i < nc))
        def _():
            b_step(i - 1)

        @pl.when(i == nc)
        def _():
            loop(0, 2, b_part)

        loop(jnp.minimum(2 * (AHEAD + 2 * i), 2 * nc), jnp.minimum(2 * (AHEAD + 2 * i + 2), 2 * nc), units)

        mine = (i == nc - 2).astype(jnp.int32)
        loop(
            before, now + 2 * mine, lambda c: loop(0, 2 - mine, lambda who: g_part(c, who, 0, tok))
        )

        @pl.when((i == nc - 4) | (i == nc - 3))
        def _():
            g_last(i - nc + 4)

        @pl.when((i >= 2) & (i <= nc))
        def _():
            c_step(i - 2)

        @pl.when(i == nc + 1)
        def _():
            loop(0, 2, c_part)

        @pl.when(i == nc - 2)
        def _():
            g_out(0, 0, tok)
            for j in range(2):
                store_grad(j).start()

        @pl.when(i < nc)
        def _():
            for d in range(2):
                send_own(d, i).wait_send()
                send_on(d, i).wait_send()
                send_sum(i, d).wait_send()
                send_unit(i, d).wait_send()

    loop(0, nc + 2, back_body)

    def drain(c):
        for d in range(2):
            send_far(d, c).wait_send()
            send_near(d, c).wait_send()
        store_new(c).wait()
        send_out(c).wait()

    def drain_part(part):
        for d in range(2):
            part_far(d, part).wait_send()
            part_near(d, part).wait_send()
        part_new(part).wait()
        part_out(part).wait()

    loop(0, end, drain)
    loop(0, 2, drain_part)
    for h in range(2):
        for j in range(2):
            send_heads(h, j).wait_send()
            send_grad(h, j).wait()
        store_grad(h).wait()
    send_weight.wait()


def step(by, params, push, inbox, heads, residual, cotangent, gain):
    rows, cols = params.shape
    tok = heads.shape[0]
    nc = cols // CW
    kh = 4 * rows
    anywhere = pl.BlockSpec(memory_space=pl.ANY)
    dma = pltpu.SemaphoreType.DMA
    return pl.pallas_call(
        functools.partial(step_kernel, by, heads.shape[1]),
        out_shape=(
            pltpu.VMEM(heads.shape, BF16),
            pltpu.VMEM((rows, cols), F32),
            pltpu.VMEM((rows, cols), BF16),
            pltpu.VMEM((8, 128), F32),
        ),
        in_specs=[pl.BlockSpec(memory_space=pltpu.HBM)] * 7,
        out_specs=[anywhere] * 4,
        scratch_shapes=[
            pltpu.VMEM((nc, rows, CW), F32),
            pltpu.VMEM((rows, cols), F32),
            pltpu.VMEM((tok, cols), BF16),
            pltpu.VMEM((tok, cols), BF16),
            pltpu.VMEM(gain.shape, F32),
            pltpu.SMEM((1,), F32),
            pltpu.VMEM((2 * tok, kh), BF16),
            pltpu.VMEM((kh, 2 * tok), BF16),
            pltpu.VMEM((nc, kh, CW), BF16),
            pltpu.VMEM((nc, tok, CW), F32),
            pltpu.VMEM((nc, tok, CW), BF16),
            pltpu.VMEM((nc, tok, CW), BF16),
            pltpu.VMEM((tok, 128), F32),
            pltpu.VMEM((tok, 128), F32),
            pltpu.VMEM((nc, 2 * tok, CW), BF16),
            pltpu.VMEM((nc, kh, CW), BF16),
            pltpu.VMEM((nc, rows, CW), BF16),
            pltpu.VMEM((2, nc, rows, CW), BF16),
            pltpu.VMEM((2 * kh // CW, tok, CW), F32),
            pltpu.VMEM((8, 128), F32),
            dma((nc,)), dma((7,)),
            dma((2, 2)), dma((2, 2)),
            dma((2, nc)), dma((2, nc)),
            dma((2, nc)), dma((2, nc)),
            dma((2, nc)), dma((2, nc)),
            dma((2, nc)), dma((2, nc)),
            dma((2, nc + 1)), dma((2, nc + 1)),
            dma((2, nc + 1)), dma((2, nc + 1)),
            dma((2, 2)), dma((2, 2)),
            dma((nc + 1,)), dma((nc + 1,)),
            dma((1,)), dma((1,)),
            dma((nc + 1,)), dma((2,)),
        ],
        compiler_params=pltpu.CompilerParams(
            collective_id=by.bit_length(), has_side_effects=True, vmem_limit_bytes=VMEM_MB * 2**20
        ),
        cost_estimate=pl.CostEstimate(
            flops=6 * tok * cols * heads.shape[1], bytes_accessed=20 * 2**20, transcendentals=tok
        ),
        name=f"push_sum_step_{by}",
    )(params, push, inbox, heads, residual, cotangent, gain)


def finish_kernel(g_in, n_in, box, w_in, push, inbox, grad, new, out, w_out, w_new, ov, pw, iw, ww, sem, csem):
    ww[0] = w_in[0, 0]
    steps = sem.shape[0]
    size = box.shape[0] // steps
    copies = [
        pltpu.make_async_copy(push, pw, csem.at[0]),
        pltpu.make_async_copy(inbox, iw, csem.at[1]),
        pltpu.make_async_copy(n_in, new, csem.at[2]),
        pltpu.make_async_copy(g_in, grad, csem.at[3]),
        pltpu.make_async_copy(ww, w_out, csem.at[4]),
    ]
    for copy in copies:
        copy.start()
    for k in range(steps):
        at = pl.ds(k * size, size)
        ov[at, :] = box[at, :].astype(F32)
        copies.append(pltpu.make_async_copy(ov.at[at], out.at[at], sem.at[k]))
        copies[-1].start()
        if k == 0:
            copies[0].wait()
            copies[1].wait()
            pw[0] = 0.5 * pw[0] + iw[0]
            copies.append(pltpu.make_async_copy(pw, w_new, csem.at[5]))
            copies[-1].start()
    for copy in copies[2:]:
        copy.wait()


def finish(g_in, n_in, box, w_in, push, inbox):
    rows, cols = box.shape
    anywhere = pl.BlockSpec(memory_space=pl.ANY)
    steps = 4
    return pl.pallas_call(
        finish_kernel,
        out_shape=(
            jax.ShapeDtypeStruct(g_in.shape, BF16),
            jax.ShapeDtypeStruct((rows, cols), F32),
            jax.ShapeDtypeStruct((rows, cols), F32),
            jax.ShapeDtypeStruct((1,), F32),
            jax.ShapeDtypeStruct((1,), F32),
        ),
        in_specs=[pl.BlockSpec(memory_space=pltpu.VMEM)] * 4 + [pl.BlockSpec(memory_space=pltpu.HBM)] * 2,
        out_specs=[anywhere] * 5,
        scratch_shapes=[
            pltpu.VMEM((rows, cols), F32),
            pltpu.SMEM((1,), F32),
            pltpu.SMEM((1,), F32),
            pltpu.SMEM((1,), F32),
            pltpu.SemaphoreType.DMA((steps,)),
            pltpu.SemaphoreType.DMA((6,)),
        ],
        compiler_params=pltpu.CompilerParams(vmem_limit_bytes=16 * 2**20),
        name="finish",
    )(g_in, n_in, box, w_in, push, inbox)


def whole(by, params, push, inbox, inbox_weight, heads, residual, cotangent, gain):
    g, new, box, weight = step(by, params, push, inbox, heads, residual, cotangent, gain)
    return finish(g, new, box, weight, push, inbox_weight)


def local(params, push_weight, inbox_params, inbox_weight, heads, residual, cotangent, gain, offset):
    operands = (
        params[0], push_weight, inbox_params[0], inbox_weight, heads[0], residual[0], cotangent[0], gain.reshape(-1, 128)
    )
    branches = [functools.partial(whole, 1 << bit) for bit in range(4)]
    grad, new, out, weight, new_weight = lax.switch(offset[0] >> 1, branches, *operands)
    return (new[None], new_weight, out[None], weight, grad[None])


def solution(mesh):
    block = P("rep", "fsdp", None)
    return jax.shard_map(
        local,
        mesh=mesh,
        in_specs=(block, P("rep"), block, P("rep"), block, block, block, P(), P()),
        out_specs=(block, P("rep"), block, P("rep"), block),
        check_vma=False,
    )
```
